256 devices in a mesh: seq: 64 (over z, y, core), batch: 4 (over x).
Axes of the slice: x: 4, y: 4, z: 8, core: 2. Of those that a mesh axis runs over, the one named last changes fastest.
Arguments:
- convolution_input: bfloat16 [4, 32768, 768], P('batch', 'seq'), may hold values from -16 to 16
- interval_index: int32 [4, 32768], P('batch', 'seq'), may hold values from 0 to 3, never falling along the last dimension, each value on 1 to 16384 neighbouring positions
- owner_lists: int32 [4, 16384, 1], P('batch', 'seq'), may hold values from 0 to 63; in each aligned block of 256 rows (0 to 255, 256 to 511, ..., all dimensions but the last counted through in order) at most 8 rows name the same one
- dilated_kernel_weight: bfloat16 [768, 3, 768], replicated, may hold values from -0.125 to 0.125
- proj_weight: bfloat16 [768, 1536], replicated, may hold values from -0.21875 to 0.21875
- owner_grads: bfloat16 [4, 64, 64, 8, 1536], P('batch', 'seq'), may hold values from -6 to 6
Outputs:
- owner_rows: bfloat16 [4, 64, 64, 8, 1536], P('batch', 'seq')
- input_grad: bfloat16 [4, 32768, 768], P('batch', 'seq')
- conv_grad: float32 [768, 3, 768], P('seq')
The draws below stay inside these ranges and needn't reach their ends.
Inputs may be any that keep to these rules, and one draw needn't show every extreme that they name: `interval_index`: positions of one interval are contiguous, ids never fall along a row. `owner_lists`: among the 256 token rows of one device, at most 8 name the same owner, and 8 is reached.
All inputs are finite; a program needn't handle non-finite values.
Results may differ from the reference program's by a relative error of at most 0.018.
Values may be sent and summed in bfloat16 or wider, within the bound.
No kernel may reach another device: no remote copies, remote signals or barrier semaphores. Data moves between devices by JAX's collectives and lax.ppermute only.
A program may use at most 128 MiB of HBM per device.

```python
import math
import jax
import jax.numpy as jnp
import numpy as np
from jax import lax

CONV_CHANNELS = 768
DT = 1536
DILATION_STEP = 32
SEGS = 4
TOK_DEV = 256
CAP = 8
ROW_LENGTH = 32768
TOKENS = 16384
SEG_MOST = 16384
BATCH = 4
N_SEQ = 64


def with_spikes(drawn, key, source, target, blocks, factor):
    owner, partner = [(jnp.arange(drawn.shape[axis_at]) // (drawn.shape[axis_at] // blocks)).reshape([-1 if axis == axis_at else 1 for axis in range(drawn.ndim)]) for axis_at in (source, target)]
    chosen = jax.random.permutation(key, blocks)[partner]
    strong = (owner == chosen) | (owner == (partner + blocks // 2) % blocks)
    return jnp.where(strong, factor * drawn, drawn)


def steps_of(rng, extent, split, smallest, largest):
    gain, own = 1.0, jax.random.fold_in(rng, 6)
    for position, parts in split:
        draws = jnp.exp(jax.random.uniform(jax.random.fold_in(own, position), (parts,), jnp.float32, smallest / len(split), largest / len(split)))
        gain = gain * jnp.repeat(draws, extent[position] // parts).reshape([-1 if axis == position else 1 for axis in range(len(extent))])
    return gain


def length_profile(number_of, total, most, slope):
    weights = [(1 << 20) // math.isqrt(grade ** slope) + 1 for grade in range(2, number_of + 1)]
    surplus, given = total - most - (number_of - 1), [1] * (number_of - 1)
    while surplus > 0:
        free = [i for i in range(number_of - 1) if given[i] < most]
        pool, left = sum([weights[i] for i in free]), surplus
        for i in free:
            more = min(most - given[i], max(1, left * weights[i] // pool), surplus)
            given[i] = given[i] + more
            surplus = surplus - more
    return np.array([most] + given)


def uneven(rng, count, total, limit, slope):
    if count == 2:
        one = jax.random.randint(rng, (), max(1, total - limit), min(limit, total - 1) + 1)
        return jnp.stack([one, total - one])
    tallies = jnp.asarray(length_profile(count, total, limit, slope), jnp.int32)
    pairs = (count - 1) // 2
    giver, sink = tallies[1:1 + 2 * pairs:2], tallies[2:2 + 2 * pairs:2]
    margin = jnp.minimum(giver - 1, limit - sink)
    shifted = jax.random.randint(jax.random.fold_in(rng, 1), (pairs,), 0, 1 << 20) % (margin + 1)
    tallies = tallies.at[1:1 + 2 * pairs:2].set(giver - shifted).at[2:2 + 2 * pairs:2].set(sink + shifted)
    return tallies[jax.random.permutation(jax.random.fold_in(rng, 2), count)]


def shared_out(key, own, number, rows, count, top, most, skew):
    order = jax.random.permutation(key, count)
    crowded, ordinary = load_shares(count, rows * top, most, skew, True), load_shares(count, rows * top, most, skew, False)
    places = jnp.arange(count)

    def named(lengths, offset_by):
        used = int((lengths > 0).sum())
        fixed = max(1, used // 4)
        shifted = fixed + (places - fixed + offset_by * (used - fixed)) % max(1, count - fixed)
        return jnp.zeros((count,), jnp.int32).at[order[jnp.where(places < fixed, places, shifted)]].set(jnp.asarray(lengths, jnp.int32))

    lengths = jnp.where(number % 4 == 0, named(crowded, number // 4), named(ordinary, number - number // 4 - 1))
    mixed = jax.random.permutation(jax.random.fold_in(own, 3), count)
    giver, sink = mixed[0:count // 2 * 2:2], mixed[1:count // 2 * 2:2]
    room = jnp.minimum(lengths[giver] - 1, most - lengths[sink]) // 2
    room = jnp.where((giver == order[0]) | (sink == order[0]) | (lengths[sink] == 0), 0, jnp.maximum(room, 0))
    shifted = jax.random.randint(jax.random.fold_in(own, 4), (count // 2,), 0, 1 << 20) % (room + 1)
    lengths = lengths.at[giver].add(-shifted).at[sink].add(shifted)
    members = jnp.searchsorted(jnp.cumsum(lengths), jnp.arange(rows * top), side="right").astype(jnp.int32)
    grid = members.reshape(top, rows).T
    grid = grid[jax.random.permutation(jax.random.fold_in(own, 1), rows)]
    offset_by = jax.random.randint(jax.random.fold_in(own, 2), (rows, 1), 0, top)
    return jnp.take_along_axis(grid, (jnp.arange(top)[None, :] + offset_by) % top, axis=1)


def load_shares(count, total, reach, skew, full):
    loads = [(1 << 20) // math.isqrt(standing ** skew) + 1 for standing in range(1, count + 1)]
    largest = reach if full else min(reach, max(-(-total // count), total * loads[0] // sum(loads)))
    least = 1 if total - largest >= count - 1 else 0
    holding, spare = [largest] + [least] * (count - 1), total - largest - least * (count - 1)
    while spare > 0:
        free = [i for i in range(1, count) if holding[i] < largest] or [i for i in range(1, count) if holding[i] < reach]
        mass, left = sum([loads[i] for i in free]), spare
        for i in free:
            extra = min(reach - holding[i], max(1, left * loads[i] // mass), spare)
            holding[i] = holding[i] + extra
            spare = spare - extra
    return np.array(holding)


def noise(own_key, shape, scale, most, split=(), kind=jnp.bfloat16):
    values = jax.random.normal(own_key, shape, jnp.float32) * scale
    if len(split) > 0:
        values = steps_of(own_key, shape, split, -0.22, 0.18) * values
    return jnp.clip(values, min=-most, max=most).astype(kind)


def bell_draw_with(rng, dims, width, reach, shards, heavy, kind=jnp.bfloat16):
    entries = width * jax.random.normal(rng, dims, jnp.float32)
    if shards:
        entries = entries * steps_of(rng, dims, shards, -0.22, 0.18)
    return jnp.clip(with_spikes(entries, jax.random.fold_in(rng, 3), *heavy), -reach, reach).astype(kind)


def setup_inputs(seed: int = 0) -> dict:
    key_list = jax.random.split(jax.random.key(seed), 7)
    convolution_input = bell_draw_with(key_list[0], (BATCH, ROW_LENGTH, CONV_CHANNELS), 1.0, 16.0, ((0, 4), (1, 64)), (1, 2, 64, 4.0))
    interval_index = jax.vmap(lambda own: jnp.searchsorted(jnp.cumsum(uneven(own, SEGS, ROW_LENGTH, SEG_MOST, 2)), jnp.arange(ROW_LENGTH), side="right"))(jax.random.split(key_list[1], BATCH)).reshape((BATCH, ROW_LENGTH)).astype(jnp.int32)
    owner_lists_keys = jax.random.split(jax.random.fold_in(key_list[2], 1), BATCH * TOKENS // TOK_DEV)
    owner_lists_turns = jax.random.permutation(jax.random.fold_in(key_list[2], 3), BATCH * TOKENS // TOK_DEV)
    owner_lists = jax.vmap(lambda own, number: shared_out(jax.random.fold_in(key_list[2], 2), own, number, TOK_DEV, N_SEQ, 1, CAP, 2))(owner_lists_keys, owner_lists_turns).reshape((BATCH, TOKENS, 1))
    dilated_kernel_weight = noise(key_list[3], (CONV_CHANNELS, 3, CONV_CHANNELS), (3 * CONV_CHANNELS) ** -0.5, 0.125)
    proj_weight = noise(key_list[4], (CONV_CHANNELS, DT), CONV_CHANNELS ** -0.5, 0.21875)
    owner_grads = noise(key_list[5], (BATCH, N_SEQ, N_SEQ, CAP, DT), 1.0, 6.0, ((0, 4), (1, 64)))
    return dict(convolution_input=convolution_input, interval_index=interval_index, owner_lists=owner_lists, dilated_kernel_weight=dilated_kernel_weight, proj_weight=proj_weight, owner_grads=owner_grads)


def gelu_exact(value):
    return 0.5 * value * (1.0 + jax.scipy.special.erf(value * 0.7071067811865476))


def gelu_slope(value):
    return 0.5 * (1.0 + jax.scipy.special.erf(value * 0.7071067811865476)) + value * jnp.exp(-0.5 * value * value) * 0.3989422804014327


def reference(convolution_input, interval_index, owner_lists, dilated_kernel_weight, proj_weight, owner_grads):
    tap_shifts = (-DILATION_STEP, 0, DILATION_STEP)
    flat_weight = dilated_kernel_weight.reshape(CONV_CHANNELS, 3 * CONV_CHANNELS)

    def forward_row(packed):
        feature_values, interval_labels = packed
        input_with_margin = jnp.pad(feature_values, ((DILATION_STEP, DILATION_STEP), (0, 0)))
        segment_with_margin = jnp.pad(interval_labels, (DILATION_STEP, DILATION_STEP), constant_values=-1)
        tap_products = jnp.dot(input_with_margin, flat_weight, preferred_element_type=jnp.float32)
        preact = jnp.zeros((ROW_LENGTH, CONV_CHANNELS), jnp.float32)
        for kernel_tap_index in range(3):
            tap_shift = tap_shifts[kernel_tap_index]
            segment_match = segment_with_margin[DILATION_STEP + tap_shift:DILATION_STEP + tap_shift + ROW_LENGTH] == interval_labels
            window_slice = tap_products[DILATION_STEP + tap_shift:DILATION_STEP + tap_shift + ROW_LENGTH, kernel_tap_index * CONV_CHANNELS:(kernel_tap_index + 1) * CONV_CHANNELS]
            preact = preact + jnp.where(segment_match[:, None], window_slice, jnp.float32(0.0))
        hidden = (feature_values.astype(jnp.float32) + gelu_exact(preact)).astype(jnp.bfloat16)
        pooled = (jnp.sum(hidden.reshape(ROW_LENGTH // 2, 2, CONV_CHANNELS).astype(jnp.float32), axis=1) * 0.5).astype(jnp.bfloat16)
        return preact, pooled

    preact_all, pooled_all = lax.map(forward_row, (convolution_input, interval_index))

    owners = owner_lists[..., 0].reshape(BATCH, N_SEQ, TOK_DEV)
    onehot = (owners[..., None] == jnp.arange(N_SEQ, dtype=jnp.int32)).astype(jnp.int32)
    slot_rank = jnp.sum((jnp.cumsum(onehot, axis=2) - onehot) * onehot, axis=-1).astype(jnp.int32)
    projected = jnp.dot(pooled_all.reshape(BATCH * TOKENS, CONV_CHANNELS), proj_weight, preferred_element_type=jnp.float32)
    projected = projected.astype(jnp.bfloat16).reshape(BATCH, N_SEQ, TOK_DEV, DT)
    batch_index = jnp.arange(BATCH, dtype=jnp.int32)[:, None, None]
    source_index = jnp.arange(N_SEQ, dtype=jnp.int32)[None, :, None]
    owner_rows = jnp.zeros((BATCH, N_SEQ, N_SEQ, CAP, DT), jnp.bfloat16)
    owner_rows = owner_rows.at[batch_index, owners, source_index, slot_rank].set(projected)
    picked = owner_grads[batch_index, owners, source_index, slot_rank]
    token_grad = jnp.dot(picked.reshape(BATCH * TOKENS, DT), proj_weight.T, preferred_element_type=jnp.float32)
    token_grad = token_grad.astype(jnp.bfloat16).reshape(BATCH, TOKENS, CONV_CHANNELS)

    def backward_row(packed):
        feature_values, interval_labels, preact, tok_grad = packed
        input_with_margin = jnp.pad(feature_values, ((DILATION_STEP, DILATION_STEP), (0, 0)))
        segment_with_margin = jnp.pad(interval_labels, (DILATION_STEP, DILATION_STEP), constant_values=-1)
        hidden_grad = jnp.repeat(tok_grad.astype(jnp.float32) * 0.5, 2, axis=0)
        preactivation_gradient = (hidden_grad * gelu_slope(preact)).astype(jnp.bfloat16)
        gradient_with_margin = jnp.pad(preactivation_gradient, ((DILATION_STEP, DILATION_STEP), (0, 0)))
        input_grad = hidden_grad
        kernel_taps = []
        for kernel_tap_index in range(3):
            tap_shift = tap_shifts[kernel_tap_index]
            forward_match = segment_with_margin[DILATION_STEP + tap_shift:DILATION_STEP + tap_shift + ROW_LENGTH] == interval_labels
            backward_match = segment_with_margin[DILATION_STEP - tap_shift:DILATION_STEP - tap_shift + ROW_LENGTH] == interval_labels
            shifted_rows = jnp.dot(gradient_with_margin[DILATION_STEP - tap_shift:DILATION_STEP - tap_shift + ROW_LENGTH], dilated_kernel_weight[:, kernel_tap_index, :].T, preferred_element_type=jnp.float32)
            input_grad = input_grad + jnp.where(backward_match[:, None], shifted_rows, jnp.float32(0.0))
            masked_terms = jnp.where(forward_match[:, None], preactivation_gradient, jnp.zeros_like(preactivation_gradient))
            kernel_taps.append(jnp.dot(input_with_margin[DILATION_STEP + tap_shift:DILATION_STEP + tap_shift + ROW_LENGTH].T, masked_terms, preferred_element_type=jnp.float32))
        return input_grad.astype(jnp.bfloat16), jnp.stack(kernel_taps, axis=1)

    input_grad, grad_rows = lax.map(backward_row, (convolution_input, interval_index, preact_all, token_grad))
    conv_grad = jnp.sum(grad_rows, axis=0)
    return owner_rows, input_grad, conv_grad
```

```python
import jax
import jax.numpy as jnp
import numpy as np
from jax import lax
from jax.sharding import Mesh, PartitionSpec as P

DIL = 32
SEQ = ("z", "y", "core")
BF = jnp.bfloat16
F32 = jnp.float32


def gelu_exact(value):
    return 0.5 * value * (1.0 + jax.scipy.special.erf(value * 0.7071067811865476))


def gelu_slope(value):
    return (
        0.5 * (1.0 + jax.scipy.special.erf(value * 0.7071067811865476))
        + value * jnp.exp(-0.5 * value * value) * 0.3989422804014327
    )


def seq_shift(array, sizes, step):
    count = int(np.prod(sizes))
    if step > 0:
        pairs = [(i, i + 1) for i in range(count - 1)]
    else:
        pairs = [(i + 1, i) for i in range(count - 1)]
    return lax.ppermute(array, SEQ, pairs)


def exchange_sum(parts, axis):
    moved = lax.all_to_all(parts, axis, 0, 0, tiled=True)
    return jnp.sum(moved.astype(F32), axis=0)


def body(x, ids, owners, weight, proj, grads):
    nz, ny, nc, nx = (lax.axis_size(a) for a in ("z", "y", "core", "batch"))
    x, ids, owners, grads = x[0], ids[0], owners[0, :, 0], grads[0, 0]
    rows, ch = x.shape
    tokens = owners.shape[0]
    devs, cap, wide = grads.shape
    slots_n = devs * cap
    core = lax.axis_index("core")
    sizes = (nz, ny, nc)
    back = jnp.dot(grads.reshape(slots_n, wide), proj.T, preferred_element_type=F32).astype(BF)
    returned = lax.all_to_all(back, SEQ, 0, 0, tiled=True)
    x_ext = jnp.concatenate(
        [seq_shift(x[-DIL:], sizes, 1), x, seq_shift(x[:DIL], sizes, -1)], axis=0
    )
    seq_idx = lax.axis_index(SEQ)
    before = jnp.where(seq_idx == 0, -1, seq_shift(ids[-DIL:], sizes, 1))
    after = jnp.where(seq_idx == devs - 1, -1, seq_shift(ids[:DIL], sizes, -1))
    ids_ext = jnp.concatenate([before, ids, after])
    same = [ids_ext[o : o + rows] == ids for o in (0, DIL, 2 * DIL)]
    w3 = weight.transpose(1, 0, 2)
    zero = jnp.zeros((), BF)
    taps = [jnp.where(same[k][:, None], x_ext[k * DIL : k * DIL + rows], zero) for k in range(3)]
    preact = jnp.dot(
        jnp.concatenate(taps, axis=1), w3.reshape(3 * ch, ch), preferred_element_type=F32
    )
    hidden = (x.astype(F32) + gelu_exact(preact)).astype(BF)
    earlier = jnp.arange(tokens)[None, :] < jnp.arange(tokens)[:, None]
    rank = jnp.sum(((owners[:, None] == owners[None, :]) & earlier).astype(jnp.int32), axis=1)
    slot = owners * cap + rank
    pick = (slot[:, None] == jnp.arange(slots_n)[None, :]).astype(BF)
    pair = jnp.where(
        (jnp.arange(rows)[None, :] // 2) == jnp.arange(tokens)[:, None], 0.5, 0.0
    ).astype(BF)
    pooled = jnp.dot(pair, hidden, preferred_element_type=F32).astype(BF)
    placed = jnp.dot(pick.T, pooled, preferred_element_type=F32).astype(BF)
    received = lax.all_to_all(placed, SEQ, 0, 0, tiled=True)
    owner_rows = jnp.dot(received, proj, preferred_element_type=F32).astype(BF)
    token_grad = jnp.dot(pick, returned, preferred_element_type=F32).astype(BF)
    hidden_grad = jnp.dot(pair.T, token_grad, preferred_element_type=F32)
    pre_grad = (hidden_grad * gelu_slope(preact)).astype(BF)
    g_ext = jnp.concatenate(
        [seq_shift(pre_grad[-DIL:], sizes, 1), pre_grad, seq_shift(pre_grad[:DIL], sizes, -1)],
        axis=0,
    )
    g_taps = [
        jnp.where(same[2 - k][:, None], g_ext[(2 - k) * DIL : (2 - k) * DIL + rows], zero)
        for k in range(3)
    ]
    input_grad = hidden_grad
    for k in range(3):
        input_grad = input_grad + jnp.dot(g_taps[k], w3[k].T, preferred_element_type=F32)
    own = ch // devs
    rest = own // nx
    order = np.arange(ch).reshape(nz, ny, nc, nx, rest).transpose(2, 3, 1, 0, 4).reshape(ch)
    perm = jnp.asarray(np.eye(ch, dtype=np.float32)[:, order], BF)
    parts = [
        lax.dot_general(
            jnp.dot(taps[k], perm, preferred_element_type=F32).astype(BF),
            pre_grad,
            (((0,), (0,)), ((), ())),
            preferred_element_type=F32,
        )
        for k in range(3)
    ]
    half = ch // 2
    total = jnp.stack(parts, axis=0).reshape(3, nc, half, ch)
    mine = lax.dynamic_index_in_dim(total, core, 1, False)
    other = lax.dynamic_index_in_dim(total, 1 - core, 1, False).astype(BF)
    chip = (mine + lax.ppermute(other, "core", [(0, 1), (1, 0)]).astype(F32)).astype(BF)
    chip = chip.reshape(3, nx, half // nx, ch).transpose(1, 0, 2, 3)
    by_x = exchange_sum(chip, "batch").astype(BF)
    by_x = by_x.reshape(3, ny, half // nx // ny, ch).transpose(1, 0, 2, 3)
    by_y = exchange_sum(by_x, "y").astype(BF)
    by_y = by_y.reshape(3, nz, rest, ch).transpose(1, 0, 2, 3)
    by_z = exchange_sum(by_y, "z").astype(BF)
    everyone = lax.all_gather(by_z, "batch", axis=0, tiled=False)
    conv_grad = everyone.transpose(0, 2, 1, 3).reshape(own, 3, ch).astype(F32)
    return (
        owner_rows.reshape(1, 1, devs, cap, wide),
        input_grad.astype(BF)[None],
        conv_grad,
    )


def solution(mesh):
    fine = Mesh(mesh.devices.reshape(8, 4, 2, 4), ("z", "y", "core", "batch"))
    return jax.shard_map(
        body,
        mesh=fine,
        in_specs=(
            P("batch", SEQ, None),
            P("batch", SEQ),
            P("batch", SEQ, None),
            P(),
            P(),
            P("batch", SEQ, None, None, None),
        ),
        out_specs=(
            P("batch", SEQ, None, None, None),
            P("batch", SEQ, None),
            P(SEQ, None, None),
        ),
        check_vma=False,
    )
```

```python
import functools

import jax
import jax.numpy as jnp
import numpy as np
from jax import lax
from jax.experimental import pallas as pl
from jax.experimental.pallas import tpu as pltpu
from jax.sharding import Mesh, PartitionSpec as P

DIL = 32
SEQ = ("z", "y", "core")
BF = jnp.bfloat16
F32 = jnp.float32
I32 = jnp.int32
LANES = 128
CHUNK = 256
NZ, NY, NC, NX = 8, 4, 2, 4
ROWS, TOKENS, SLOTS, CH, WIDE, CAP = 512, 256, 512, 768, 1536, 8
HALF = CH // 2
OWN = CH // (NZ * NY * NC)
REST = OWN // NX
PIECE = NZ * REST
VMEM = 60 * 1024 * 1024
SMEM_SPEC = pl.BlockSpec(memory_space=pltpu.SMEM)


def nt_dot(a, b):
    return lax.dot_general(a, b, (((1,), (1,)), ((), ())), preferred_element_type=F32)


def tn_dot(a, b):
    return lax.dot_general(a, b, (((0,), (0,)), ((), ())), preferred_element_type=F32)


def dot(a, b):
    return jnp.dot(a, b, preferred_element_type=F32)


def whole(shape):
    return pl.BlockSpec(shape, lambda j: (0,) * len(shape))


def iota(shape, dim):
    return lax.broadcasted_iota(I32, shape, dim)


def channel_order(core, x_me, y_me):
    q = iota((CH, LANES), 0)
    other = (q >= HALF).astype(I32)
    left = q - HALF * other
    parts = []
    size = HALF
    for count in (NY, NX, NZ):
        size //= count
        digit = jnp.zeros_like(q)
        for i in range(1, count):
            digit += (left >= size * i).astype(I32)
        left = left - size * digit
        parts.append(digit)
    y, x, z = parts
    half = core + other - 2 * core * other
    y, x = y + y_me, x + x_me
    y = jnp.where(y >= NY, y - NY, y)
    x = jnp.where(x >= NX, x - NX, x)
    return z * (NY * NC * OWN) + y * (NC * OWN) + half * OWN + x * REST + left


def forward_kernel(
    place_ref, x_ref, peer_ref, out_ref, ids_ref, own_ref, w_ref,
    slope_ref, placed_ref, xt_mine_ref, xt_peer_ref, pick_ref, mask_ref,
    taps, perm, pick_t, pair,
):
    j = pl.program_id(0)
    core = place_ref[0]

    @pl.when(j == 0)
    def _():
        first = core == 0
        before = jnp.where(first, out_ref[...], peer_ref[...])
        after = jnp.where(first, peer_ref[...], out_ref[...])
        ids_col = jnp.transpose(
            jnp.broadcast_to(ids_ref[...].astype(F32), (LANES, ROWS)), (1, 0)
        )
        ids_ext = jnp.concatenate(
            [before[:, CH:].astype(F32), ids_col, after[:, CH:].astype(F32)], axis=0
        )
        x_ext = jnp.concatenate([before[:, :CH], x_ref[...], after[:, :CH]], axis=0)
        taps[1] = x_ref[...]
        for i, k in ((0, 0), (1, 2)):
            same = jnp.where(ids_ext[k * DIL : k * DIL + ROWS] == ids_col, 1.0, 0.0).astype(BF)
            mask_ref[i] = same
            for c in range(0, CH, LANES):
                taps[k, :, c : c + LANES] = x_ext[k * DIL : k * DIL + ROWS, c : c + LANES] * same
        order = channel_order(core, place_ref[1], place_ref[2])
        for c in range(0, CH, LANES):
            perm[:, c : c + LANES] = jnp.where(
                order == iota((CH, LANES), 1) + c, 1.0, 0.0
            ).astype(BF)
        own_row = own_ref[...].astype(F32)
        row_b = jnp.broadcast_to(own_row, (TOKENS, TOKENS))
        col_b = jnp.transpose(row_b, (1, 0))
        src, dst = iota((TOKENS, TOKENS), 0), iota((TOKENS, TOKENS), 1)
        earlier = jnp.where((row_b == col_b) & (src < dst), 1.0, 0.0)
        slot_row = (own_row * CAP + jnp.sum(earlier, axis=0, keepdims=True)).astype(I32)
        pick_t[...] = jnp.where(iota((SLOTS, TOKENS), 0) == slot_row, 1.0, 0.0).astype(BF)
        two = 2 * iota((TOKENS, ROWS), 0)
        pos = iota((TOKENS, ROWS), 1)
        pair[...] = jnp.where((pos == two) | (pos == two + 1), 0.5, 0.0).astype(BF)
        pick_ref[...] = lax.dot_general(
            pair[...], pick_t[...], (((0,), (1,)), ((), ())), preferred_element_type=F32
        ).astype(BF)

    preact = dot(taps[0], w_ref[0]) + dot(taps[1], w_ref[1]) + dot(taps[2], w_ref[2])
    cdf = 0.5 * (1.0 + lax.erf(preact * 0.7071067811865476))
    slope_ref[...] = cdf + preact * jnp.exp(-0.5 * preact * preact) * 0.3989422804014327
    x_own = x_ref[:, pl.ds(pl.multiple_of(j * CHUNK, CHUNK), CHUNK)].astype(F32)
    hidden = (x_own + preact * cdf).astype(BF)
    pooled = dot(pair[...], hidden).astype(BF)
    placed_ref[...] = dot(pick_t[...], pooled).astype(BF)
    turned = nt_dot(perm[...], taps[j]).astype(BF)
    xt_mine_ref[0] = turned[:HALF]
    xt_peer_ref[0] = turned[HALF:]


def forward(place, x, peer, out, ids, own, w3):
    col = lambda j: (0, j)
    tap = lambda j: (j, 0, 0)
    halo = (DIL, CH + LANES)
    return pl.pallas_call(
        forward_kernel,
        grid=(3,),
        in_specs=[
            SMEM_SPEC, whole((ROWS, CH)), whole(halo), whole(halo), whole((1, ROWS)),
            whole((1, TOKENS)), pl.BlockSpec((3, CH, CHUNK), lambda j: (0, 0, j)),
        ],
        out_specs=[
            pl.BlockSpec((ROWS, CHUNK), col), pl.BlockSpec((SLOTS, CHUNK), col),
            pl.BlockSpec((1, HALF, ROWS), tap), pl.BlockSpec((1, HALF, ROWS), tap),
            whole((ROWS, SLOTS)), whole((2, ROWS, LANES)),
        ],
        out_shape=[
            jax.ShapeDtypeStruct((ROWS, CH), F32), jax.ShapeDtypeStruct((SLOTS, CH), BF),
            jax.ShapeDtypeStruct((3, HALF, ROWS), BF), jax.ShapeDtypeStruct((3, HALF, ROWS), BF),
            jax.ShapeDtypeStruct((ROWS, SLOTS), BF), jax.ShapeDtypeStruct((2, ROWS, LANES), BF),
        ],
        scratch_shapes=[
            pltpu.VMEM((3, ROWS, CH), BF), pltpu.VMEM((CH, CH), BF), pltpu.VMEM((SLOTS, TOKENS), BF),
            pltpu.VMEM((TOKENS, ROWS), BF),
        ],
        compiler_params=pltpu.CompilerParams(vmem_limit_bytes=VMEM),
        name="forward",
    )(place, x, peer, out, ids, own, w3)


def grad_kernel(ret_ref, pick_ref, slope_ref, g_ref):
    g_ref[...] = (dot(pick_ref[...], ret_ref[...]) * slope_ref[...]).astype(BF)


def gradient(returned, pick, slope):
    col = lambda j: (0, j)
    return pl.pallas_call(
        grad_kernel,
        grid=(CH // CHUNK,),
        in_specs=[
            pl.BlockSpec((SLOTS, CHUNK), col), whole((ROWS, SLOTS)), pl.BlockSpec((ROWS, CHUNK), col),
        ],
        out_specs=pl.BlockSpec((ROWS, CHUNK), col),
        out_shape=jax.ShapeDtypeStruct((ROWS, CH), BF),
        compiler_params=pltpu.CompilerParams(vmem_limit_bytes=VMEM),
        name="gradient",
    )(returned, pick, slope)


def wgrad_kernel(mine_ref, peer_ref, g_ref, gp_ref, *refs):
    total = dot(mine_ref[0], g_ref[...]) + dot(peer_ref[0], gp_ref[...])
    for i in range(NY):
        for d in range(NX):
            low = (i * NX + d) * PIECE
            block = total[low : low + PIECE].astype(BF)
            refs[d][0, i] = block[:, :HALF]
            refs[NX + i][0, d] = block[:, HALF:]


def wgrad(mine, peer, g, gp):
    tap = lambda j: (j, 0, 0)
    out = jax.ShapeDtypeStruct((3, NY, PIECE, HALF), BF)
    spec = pl.BlockSpec((1, NY, PIECE, HALF), lambda j: (j, 0, 0, 0))
    outs = pl.pallas_call(
        wgrad_kernel,
        grid=(3,),
        in_specs=[
            pl.BlockSpec((1, HALF, ROWS), tap), pl.BlockSpec((1, HALF, ROWS), tap),
            whole((ROWS, CH)), whole((ROWS, CH)),
        ],
        out_specs=[spec] * (NX + NY),
        out_shape=[out] * (NX + NY),
        compiler_params=pltpu.CompilerParams(vmem_limit_bytes=VMEM),
        name="wgrad",
    )(mine, peer, g, gp)
    return outs[:NX], outs[NX:]


def sum_kernel(*refs):
    for side in (0, 1):
        ins = refs[4 * side : 4 * side + 4]
        for d in range(4):
            total = ins[0][0, d].astype(F32)
            for ref in ins[1:]:
                total += ref[0, d].astype(F32)
            refs[8 + 4 * side + d][0] = total.astype(BF)


def sum_parts(a_parts, b_parts):
    ins = pl.BlockSpec((1, 4, PIECE, HALF), lambda j: (j, 0, 0, 0))
    outs = pl.BlockSpec((1, PIECE, HALF), lambda j: (j, 0, 0))
    got = pl.pallas_call(
        sum_kernel,
        grid=(3,),
        in_specs=[ins] * 8,
        out_specs=[outs] * 8,
        out_shape=[jax.ShapeDtypeStruct((3, PIECE, HALF), BF)] * 8,
        compiler_params=pltpu.CompilerParams(vmem_limit_bytes=VMEM),
        name="sum_parts",
    )(*a_parts, *b_parts)
    return got[:4], got[4:]


def dgrad_kernel(place_ref, g_ref, gp_ref, out_ref, mask_ref, pick_ref, ret_ref, w_ref, o_ref, taps):
    @pl.when(pl.program_id(0) == 0)
    def _():
        first = place_ref[0] == 0
        before = jnp.where(first, out_ref[...], gp_ref[ROWS - DIL :])
        after = jnp.where(first, gp_ref[:DIL], out_ref[...])
        g_ext = jnp.concatenate([before, g_ref[...], after], axis=0)
        for i, k in ((0, 2), (1, 0)):
            low = (2 - k) * DIL
            for c in range(0, CH, LANES):
                taps[i, :, c : c + LANES] = g_ext[low : low + ROWS, c : c + LANES] * mask_ref[i]

    total = dot(pick_ref[...], ret_ref[...])
    total += nt_dot(taps[1], w_ref[0])
    total += nt_dot(g_ref[...], w_ref[1])
    total += nt_dot(taps[0], w_ref[2])
    o_ref[...] = total.astype(BF)


def dgrad(place, g, gp, out, masks, pick, returned, w3):
    col = lambda j: (0, j)
    return pl.pallas_call(
        dgrad_kernel,
        grid=(CH // CHUNK,),
        in_specs=[
            SMEM_SPEC, whole((ROWS, CH)), whole((ROWS, CH)), whole((DIL, CH)),
            whole((2, ROWS, LANES)), whole((ROWS, SLOTS)), pl.BlockSpec((SLOTS, CHUNK), col),
            pl.BlockSpec((3, CHUNK, CH), lambda j: (0, j, 0)),
        ],
        out_specs=pl.BlockSpec((ROWS, CHUNK), col),
        out_shape=jax.ShapeDtypeStruct((ROWS, CH), BF),
        scratch_shapes=[pltpu.VMEM((2, ROWS, CH), BF)],
        compiler_params=pltpu.CompilerParams(vmem_limit_bytes=VMEM),
        name="dgrad",
    )(place, g, gp, out, masks, pick, returned, w3)


def to_peer(array):
    return lax.ppermute(array, "core", [(0, 1), (1, 0)])


def to_next_chip(array):
    last = NZ * NY * NC
    pairs = [(i, i - 1) for i in range(2, last, 2)] + [(i, i + 1) for i in range(1, last - 1, 2)]
    return lax.ppermute(array, SEQ, pairs)


def spread(pieces, axis):
    count = len(pieces)
    got = [pieces[0]]
    for d in range(1, count):
        pairs = [(i, (i + d) % count) for i in range(count)]
        got.append(lax.ppermute(pieces[d], axis, pairs))
    return got


def gather_x(array):
    me = lax.axis_index("batch")
    stacked = jnp.stack(spread([array] * NX, "batch"), axis=0)
    return [
        lax.dynamic_index_in_dim(stacked, (me - i + NX) % NX, 0, False) for i in range(NX)
    ]


def body(x, ids, owners, weight, proj, grads):
    x, ids, owners, grads = x[0], ids[0], owners[0, :, 0], grads[0, 0]
    core = lax.axis_index("core")
    first = core == 0
    place = jnp.stack([core, lax.axis_index("batch"), lax.axis_index("y")]).astype(I32)
    ids_b = ids.astype(BF)
    head = jnp.concatenate([x[:DIL], jnp.broadcast_to(ids_b[:DIL, None], (DIL, LANES))], axis=1)
    tail = jnp.concatenate([x[-DIL:], jnp.broadcast_to(ids_b[-DIL:, None], (DIL, LANES))], axis=1)
    peer_halo = to_peer(jnp.where(first, tail, head))
    out_halo = to_next_chip(jnp.where(first, head, tail))
    back = jnp.dot(grads.reshape(SLOTS, WIDE), proj.T, preferred_element_type=F32).astype(BF)
    back, peer_halo, out_halo = lax.optimization_barrier((back, peer_halo, out_halo))
    returned = lax.all_to_all(back, SEQ, 0, 0, tiled=True)
    w3 = weight.transpose(1, 0, 2)
    slope, placed, xt_mine, xt_peer, pick, masks = forward(
        place, x, peer_halo, out_halo, ids[None], owners[None], w3
    )
    xt_from = to_peer(xt_peer)
    received = lax.all_to_all(placed, SEQ, 0, 0, tiled=True)
    g = gradient(returned, pick, slope)
    g_peer = to_peer(g)
    g_out = to_next_chip(jnp.where(first, g[:DIL], g[-DIL:]))
    a_parts, b_parts = wgrad(xt_mine, xt_from, g, g_peer)
    a_parts, b_parts = spread(a_parts, "batch"), spread(b_parts, "y")
    input_grad = dgrad(place, g, g_peer, g_out, masks, pick, returned, w3)
    a_next, b_next = sum_parts(a_parts, b_parts)
    a_next, b_next, received, input_grad = lax.optimization_barrier(
        (a_next, b_next, received, input_grad)
    )
    owner_rows = jnp.dot(received, proj, preferred_element_type=F32).astype(BF)
    a_next, b_next = spread(a_next, "y"), spread(b_next, "batch")
    by_xy = jnp.concatenate(
        [sum(part.astype(F32) for part in parts) for parts in (a_next, b_next)], axis=-1
    ).astype(BF)
    by_xy = by_xy.reshape(3, NZ, REST, CH).transpose(1, 0, 2, 3)
    by_xy, owner_rows = lax.optimization_barrier((by_xy, owner_rows))
    by_z = lax.all_to_all(by_xy, "z", 0, 0, tiled=True)
    by_z = jnp.sum(by_z.astype(F32), axis=0).astype(BF)
    every = jnp.concatenate(gather_x(by_z), axis=1)
    conv_grad = every.transpose(1, 0, 2).astype(F32)
    return (
        owner_rows.reshape(1, 1, NZ * NY * NC, CAP, WIDE),
        input_grad[None],
        conv_grad,
    )


def solution(mesh):
    fine = Mesh(mesh.devices.reshape(NZ, NY, NC, NX), ("z", "y", "core", "batch"))
    return jax.shard_map(
        body,
        mesh=fine,
        in_specs=(
            P("batch", SEQ, None),
            P("batch", SEQ),
            P("batch", SEQ, None),
            P(),
            P(),
            P("batch", SEQ, None, None, None),
        ),
        out_specs=(
            P("batch", SEQ, None, None, None),
            P("batch", SEQ, None),
            P(SEQ, None, None),
        ),
        check_vma=False,
    )
```

```python
import functools

import jax
import jax.numpy as jnp
import numpy as np
from jax import lax
from jax.experimental import pallas as pl
from jax.experimental.pallas import tpu as pltpu
from jax.sharding import Mesh, PartitionSpec as P

DIL = 32
SEQ = ("z", "y", "core")
BF = jnp.bfloat16
F32 = jnp.float32
I32 = jnp.int32
LANES = 128
CHUNK = 256
NZ, NY, NC, NX = 8, 4, 2, 4
ROWS, TOKENS, SLOTS, CH, WIDE, CAP = 512, 256, 512, 768, 1536, 8
HALF = CH // 2
OWN = CH // (NZ * NY * NC)
REST = OWN // NX
PIECE = NZ * REST
PART = NY * PIECE
VMEM = 20 * 1024 * 1024
SMEM_SPEC = pl.BlockSpec(memory_space=pltpu.SMEM)


def nt_dot(a, b):
    return lax.dot_general(a, b, (((1,), (1,)), ((), ())), preferred_element_type=F32)


def tn_dot(a, b):
    return lax.dot_general(a, b, (((0,), (0,)), ((), ())), preferred_element_type=F32)


def dot(a, b):
    return jnp.dot(a, b, preferred_element_type=F32)


def whole(shape):
    return pl.BlockSpec(shape, lambda j: (0,) * len(shape))


def iota(shape, dim):
    return lax.broadcasted_iota(I32, shape, dim)


def channel_order(core, x_me, y_me):
    q = iota((CH, LANES), 0)
    other = (q >= HALF).astype(I32)
    left = q - HALF * other
    parts = []
    size = HALF
    for count in (NX, NY, NZ):
        size //= count
        digit = jnp.zeros_like(q)
        for i in range(1, count):
            digit += (left >= size * i).astype(I32)
        left = left - size * digit
        parts.append(digit)
    x, y, z = parts
    half = core + other - 2 * core * other
    y, x = y + y_me, x + x_me
    y = jnp.where(y >= NY, y - NY, y)
    x = jnp.where(x >= NX, x - NX, x)
    return z * (NY * NC * OWN) + y * (NC * OWN) + half * OWN + x * REST + left


def forward_kernel(
    place_ref, x_ref, peer_ref, out_ref, ids_ref, own_ref, w_ref,
    slope_ref, placed_ref, xt_mine_ref, xt_peer_ref, pick_ref, mask_ref,
    taps, perm, pick_t, pair,
):
    j = pl.program_id(0)
    core = place_ref[0]

    @pl.when(j == 0)
    def _():
        first = core == 0
        before = jnp.where(first, out_ref[...], peer_ref[...])
        after = jnp.where(first, peer_ref[...], out_ref[...])
        ids_col = jnp.transpose(
            jnp.broadcast_to(ids_ref[...].astype(F32), (LANES, ROWS)), (1, 0)
        )
        ids_ext = jnp.concatenate(
            [before[:, CH:].astype(F32), ids_col, after[:, CH:].astype(F32)], axis=0
        )
        x_ext = jnp.concatenate([before[:, :CH], x_ref[...], after[:, :CH]], axis=0)
        taps[1] = x_ref[...]
        for i, k in ((0, 0), (1, 2)):
            same = jnp.where(ids_ext[k * DIL : k * DIL + ROWS] == ids_col, 1.0, 0.0).astype(BF)
            mask_ref[i] = same
            for c in range(0, CH, LANES):
                taps[k, :, c : c + LANES] = x_ext[k * DIL : k * DIL + ROWS, c : c + LANES] * same
        order = channel_order(core, place_ref[1], place_ref[2])
        for c in range(0, CH, LANES):
            perm[:, c : c + LANES] = jnp.where(
                order == iota((CH, LANES), 1) + c, 1.0, 0.0
            ).astype(BF)
        own_row = own_ref[...].astype(F32)
        row_b = jnp.broadcast_to(own_row, (TOKENS, TOKENS))
        col_b = jnp.transpose(row_b, (1, 0))
        src, dst = iota((TOKENS, TOKENS), 0), iota((TOKENS, TOKENS), 1)
        earlier = jnp.where((row_b == col_b) & (src < dst), 1.0, 0.0)
        slot_row = (own_row * CAP + jnp.sum(earlier, axis=0, keepdims=True)).astype(I32)
        pick_t[...] = jnp.where(iota((SLOTS, TOKENS), 0) == slot_row, 1.0, 0.0).astype(BF)
        two = 2 * iota((TOKENS, ROWS), 0)
        pos = iota((TOKENS, ROWS), 1)
        pair[...] = jnp.where((pos == two) | (pos == two + 1), 0.5, 0.0).astype(BF)
        pick_ref[...] = lax.dot_general(
            pair[...], pick_t[...], (((0,), (1,)), ((), ())), preferred_element_type=F32
        ).astype(BF)

    preact = dot(taps[0], w_ref[0]) + dot(taps[1], w_ref[1]) + dot(taps[2], w_ref[2])
    cdf = 0.5 * (1.0 + lax.erf(preact * 0.7071067811865476))
    bell = jnp.exp(-0.5 * preact * preact) * 0.3989422804014327
    slope_ref[...] = (cdf + preact * bell).astype(BF)
    x_own = x_ref[:, pl.ds(pl.multiple_of(j * CHUNK, CHUNK), CHUNK)].astype(F32)
    hidden = (x_own + preact * cdf).astype(BF)
    pooled = dot(pair[...], hidden).astype(BF)
    placed_ref[...] = dot(pick_t[...], pooled).astype(BF)
    turned = nt_dot(perm[...], taps[j]).astype(BF)
    xt_mine_ref[0] = turned[:HALF]
    xt_peer_ref[0] = turned[HALF:]


def forward(place, x, peer, out, ids, own, w3):
    col = lambda j: (0, j)
    tap = lambda j: (j, 0, 0)
    halo = (DIL, CH + LANES)
    return pl.pallas_call(
        forward_kernel,
        grid=(3,),
        in_specs=[
            SMEM_SPEC, whole((ROWS, CH)), whole(halo), whole(halo), whole((1, ROWS)),
            whole((1, TOKENS)), pl.BlockSpec((3, CH, CHUNK), lambda j: (0, 0, j)),
        ],
        out_specs=[
            pl.BlockSpec((ROWS, CHUNK), col), pl.BlockSpec((SLOTS, CHUNK), col),
            pl.BlockSpec((1, HALF, ROWS), tap), pl.BlockSpec((1, HALF, ROWS), tap),
            whole((ROWS, SLOTS)), whole((2, ROWS, LANES)),
        ],
        out_shape=[
            jax.ShapeDtypeStruct((ROWS, CH), BF), jax.ShapeDtypeStruct((SLOTS, CH), BF),
            jax.ShapeDtypeStruct((3, HALF, ROWS), BF), jax.ShapeDtypeStruct((3, HALF, ROWS), BF),
            jax.ShapeDtypeStruct((ROWS, SLOTS), BF),
            jax.ShapeDtypeStruct((2, ROWS, LANES), BF),
        ],
        scratch_shapes=[
            pltpu.VMEM((3, ROWS, CH), BF), pltpu.VMEM((CH, CH), BF), pltpu.VMEM((SLOTS, TOKENS), BF),
            pltpu.VMEM((TOKENS, ROWS), BF),
        ],
        compiler_params=pltpu.CompilerParams(vmem_limit_bytes=VMEM),
        name="forward",
    )(place, x, peer, out, ids, own, w3)


def grad_kernel(place_ref, ret_ref, pick_ref, slope_ref, g_ref, edge_ref):
    g = (dot(pick_ref[...], ret_ref[...]) * slope_ref[...].astype(F32)).astype(BF)
    g_ref[...] = g
    edge_ref[...] = jnp.where(place_ref[0] == 0, g[:DIL], g[ROWS - DIL :])


def gradient(place, returned, pick, slope):
    col = lambda j: (0, j)
    return pl.pallas_call(
        grad_kernel,
        grid=(CH // HALF,),
        in_specs=[
            SMEM_SPEC, pl.BlockSpec((SLOTS, HALF), col), whole((ROWS, SLOTS)),
            pl.BlockSpec((ROWS, HALF), col),
        ],
        out_specs=[pl.BlockSpec((ROWS, HALF), col), pl.BlockSpec((DIL, HALF), col)],
        out_shape=[jax.ShapeDtypeStruct((ROWS, CH), BF), jax.ShapeDtypeStruct((DIL, CH), BF)],
        compiler_params=pltpu.CompilerParams(vmem_limit_bytes=VMEM),
        name="gradient",
    )(place, returned, pick, slope)


def wgrad_kernel(xt_ref, xtp_ref, g_ref, gp_ref, *outs):
    for k in range(3):
        total = dot(xt_ref[k], g_ref[...]) + dot(xtp_ref[k], gp_ref[...])
        for d in range(NX):
            outs[d][k] = total[d * PART : (d + 1) * PART].astype(BF)


def wgrad(xt, xt_peer, g, gp):
    cols = pl.BlockSpec((ROWS, CHUNK), lambda j: (0, j))
    xts = whole((3, HALF, ROWS))
    return pl.pallas_call(
        wgrad_kernel,
        grid=(CH // CHUNK,),
        in_specs=[xts, xts, cols, cols],
        out_specs=[pl.BlockSpec((3, PART, CHUNK), lambda j: (0, 0, j))] * NX,
        out_shape=[jax.ShapeDtypeStruct((3, PART, CH), BF)] * NX,
        compiler_params=pltpu.CompilerParams(vmem_limit_bytes=VMEM),
        name="wgrad",
    )(xt, xt_peer, g, gp)


def sum_kernel(*refs):
    ins, outs = refs[:NX], refs[NX:]
    total = ins[0][...].astype(F32)
    for ref in ins[1:]:
        total += ref[...].astype(F32)
    for d in range(NY):
        outs[d][...] = total[:, d * PIECE : (d + 1) * PIECE].astype(BF)


def sum_parts(parts):
    return pl.pallas_call(
        sum_kernel,
        out_shape=[jax.ShapeDtypeStruct((3, PIECE, CH), BF)] * NY,
        compiler_params=pltpu.CompilerParams(vmem_limit_bytes=VMEM),
        name="sum_parts",
    )(*parts)


def dgrad_kernel(place_ref, g_ref, gp_ref, out_ref, mask_ref, pick_ref, ret_ref, w_ref, o_ref, taps):
    @pl.when(pl.program_id(0) == 0)
    def _():
        first = place_ref[0] == 0
        before = jnp.where(first, out_ref[...], gp_ref[ROWS - DIL :])
        after = jnp.where(first, gp_ref[:DIL], out_ref[...])
        g_ext = jnp.concatenate([before, g_ref[...], after], axis=0)
        for i, k in ((0, 2), (1, 0)):
            low = (2 - k) * DIL
            for c in range(0, CH, LANES):
                taps[i, :, c : c + LANES] = g_ext[low : low + ROWS, c : c + LANES] * mask_ref[i]

    total = dot(pick_ref[...], ret_ref[...])
    total += nt_dot(taps[1], w_ref[0])
    total += nt_dot(g_ref[...], w_ref[1])
    total += nt_dot(taps[0], w_ref[2])
    o_ref[...] = total.astype(BF)


def dgrad(place, g, gp, out, masks, pick, returned, w3):
    col = lambda j: (0, j)
    return pl.pallas_call(
        dgrad_kernel,
        grid=(CH // CHUNK,),
        in_specs=[
            SMEM_SPEC, whole((ROWS, CH)), whole((ROWS, CH)), whole((DIL, CH)),
            whole((2, ROWS, LANES)), whole((ROWS, SLOTS)), pl.BlockSpec((SLOTS, CHUNK), col),
            pl.BlockSpec((3, CHUNK, CH), lambda j: (0, j, 0)),
        ],
        out_specs=pl.BlockSpec((ROWS, CHUNK), col),
        out_shape=jax.ShapeDtypeStruct((ROWS, CH), BF),
        scratch_shapes=[pltpu.VMEM((2, ROWS, CH), BF)],
        compiler_params=pltpu.CompilerParams(vmem_limit_bytes=VMEM),
        name="dgrad",
    )(place, g, gp, out, masks, pick, returned, w3)


def to_peer(array):
    return lax.ppermute(array, "core", [(0, 1), (1, 0)])


def to_next_chip(array):
    last = NZ * NY * NC
    pairs = [(i, i - 1) for i in range(2, last, 2)] + [(i, i + 1) for i in range(1, last - 1, 2)]
    return lax.ppermute(array, SEQ, pairs)


def spread(pieces, axis):
    count = len(pieces)
    got = [pieces[0]]
    for d in range(1, count):
        pairs = [(i, (i + d) % count) for i in range(count)]
        got.append(lax.ppermute(pieces[d], axis, pairs))
    return got


def gather_x(array):
    me = lax.axis_index("batch")
    stacked = jnp.stack(spread([array] * NX, "batch"), axis=0)
    return [
        lax.dynamic_index_in_dim(stacked, (me - i + NX) % NX, 0, False) for i in range(NX)
    ]


def body(x, ids, owners, weight, proj, grads):
    x, ids, owners, grads = x[0], ids[0], owners[0, :, 0], grads[0, 0]
    core = lax.axis_index("core")
    first = core == 0
    place = jnp.stack([core, lax.axis_index("batch"), lax.axis_index("y")]).astype(I32)
    ids_b = ids.astype(BF)
    head = jnp.concatenate([x[:DIL], jnp.broadcast_to(ids_b[:DIL, None], (DIL, LANES))], axis=1)
    tail = jnp.concatenate([x[-DIL:], jnp.broadcast_to(ids_b[-DIL:, None], (DIL, LANES))], axis=1)
    peer_halo = to_peer(jnp.where(first, tail, head))
    out_halo = to_next_chip(jnp.where(first, head, tail))
    back = jnp.dot(grads.reshape(SLOTS, WIDE), proj.T, preferred_element_type=F32).astype(BF)
    back, peer_halo, out_halo = lax.optimization_barrier((back, peer_halo, out_halo))
    returned = lax.all_to_all(back, SEQ, 0, 0, tiled=True)
    w3 = weight.transpose(1, 0, 2)
    slope, placed, xt_mine, xt_peer, pick, masks = forward(
        place, x, peer_halo, out_halo, ids[None], owners[None], w3
    )
    xt_from = to_peer(xt_peer)
    g, edge = gradient(place, returned, pick, slope)
    g_peer = to_peer(g)
    g_out = to_next_chip(edge)
    placed, g = lax.optimization_barrier((placed, g))
    received = lax.all_to_all(placed, SEQ, 0, 0, tiled=True)
    parts = spread(wgrad(xt_mine, xt_from, g, g_peer), "batch")
    input_grad = dgrad(place, g, g_peer, g_out, masks, pick, returned, w3)
    pieces = sum_parts(parts)
    pieces, input_grad = lax.optimization_barrier((pieces, input_grad))
    pieces = spread(pieces, "y")
    by_xy = sum(part.astype(F32) for part in pieces).astype(BF)
    by_xy = by_xy.reshape(3, NZ, REST, CH).transpose(1, 0, 2, 3)
    by_xy, received = lax.optimization_barrier((by_xy, received))
    owner_rows = jnp.dot(received, proj, preferred_element_type=F32).astype(BF)
    by_z = lax.all_to_all(by_xy, "z", 0, 0, tiled=True)
    by_z = jnp.sum(by_z.astype(F32), axis=0).astype(BF)
    copies = jnp.broadcast_to(by_z[None], (NX,) + by_z.shape)
    every = lax.all_to_all(copies, "batch", 0, 0, tiled=True)
    conv_grad = every.transpose(0, 2, 1, 3).reshape(OWN, 3, CH).astype(F32)
    return (
        owner_rows.reshape(1, 1, NZ * NY * NC, CAP, WIDE),
        input_grad[None],
        conv_grad,
    )


def solution(mesh):
    fine = Mesh(mesh.devices.reshape(NZ, NY, NC, NX), ("z", "y", "core", "batch"))
    return jax.shard_map(
        body,
        mesh=fine,
        in_specs=(
            P("batch", SEQ, None),
            P("batch", SEQ),
            P("batch", SEQ, None),
            P(),
            P(),
            P("batch", SEQ, None, None, None),
        ),
        out_specs=(
            P("batch", SEQ, None, None, None),
            P("batch", SEQ, None),
            P(SEQ, None, None),
        ),
        check_vma=False,
    )
```

```python
import functools

import jax
import jax.numpy as jnp
import numpy as np
from jax import lax
from jax.experimental import pallas as pl
from jax.experimental.pallas import tpu as pltpu
from jax.sharding import Mesh, PartitionSpec as P

DIL = 32
SEQ = ("z", "y", "core")
BF = jnp.bfloat16
F32 = jnp.float32
I32 = jnp.int32
LANES = 128
CHUNK = 256
NZ, NY, NC, NX = 8, 4, 2, 4
ROWS, TOKENS, SLOTS, CH, WIDE, CAP = 512, 256, 512, 768, 1536, 8
HALF = CH // 2
OWN = CH // (NZ * NY * NC)
REST = OWN // NX
PIECE = NZ * REST
PART = NY * PIECE
VMEM = 20 * 1024 * 1024
SMEM_SPEC = pl.BlockSpec(memory_space=pltpu.SMEM)


def nt_dot(a, b):
    return lax.dot_general(a, b, (((1,), (1,)), ((), ())), preferred_element_type=F32)


def tn_dot(a, b):
    return lax.dot_general(a, b, (((0,), (0,)), ((), ())), preferred_element_type=F32)


def dot(a, b):
    return jnp.dot(a, b, preferred_element_type=F32)


def whole(shape):
    return pl.BlockSpec(shape, lambda j: (0,) * len(shape))


def iota(shape, dim):
    return lax.broadcasted_iota(I32, shape, dim)


def channel_order(core, x_me, y_me):
    q = iota((CH, LANES), 0)
    other = (q >= HALF).astype(I32)
    left = q - HALF * other
    parts = []
    size = HALF
    for count in (NX, NY, NZ):
        size //= count
        digit = jnp.zeros_like(q)
        for i in range(1, count):
            digit += (left >= size * i).astype(I32)
        left = left - size * digit
        parts.append(digit)
    x, y, z = parts
    half = core + other - 2 * core * other
    y, x = y + y_me, x + x_me
    y = jnp.where(y >= NY, y - NY, y)
    x = jnp.where(x >= NX, x - NX, x)
    return z * (NY * NC * OWN) + y * (NC * OWN) + half * OWN + x * REST + left


def forward_kernel(
    place_ref, x_ref, peer_ref, out_ref, ids_ref, own_ref, w_ref,
    both_ref, placed_ref, xt_mine_ref, xt_peer_ref, mask_ref,
    taps, perm, pick_t, pair,
):
    j = pl.program_id(0)
    core = place_ref[0]

    @pl.when(j == 0)
    def _():
        first = core == 0
        before = jnp.where(first, out_ref[...], peer_ref[...])
        after = jnp.where(first, peer_ref[...], out_ref[...])
        ids_col = jnp.transpose(
            jnp.broadcast_to(ids_ref[...].astype(F32), (LANES, ROWS)), (1, 0)
        )
        ids_ext = jnp.concatenate(
            [before[:, CH:].astype(F32), ids_col, after[:, CH:].astype(F32)], axis=0
        )
        x_ext = jnp.concatenate([before[:, :CH], x_ref[...], after[:, :CH]], axis=0)
        taps[1] = x_ref[...]
        for i, k in ((0, 0), (1, 2)):
            same = jnp.where(ids_ext[k * DIL : k * DIL + ROWS] == ids_col, 1.0, 0.0).astype(BF)
            mask_ref[i] = same
            for c in range(0, CH, LANES):
                taps[k, :, c : c + LANES] = x_ext[k * DIL : k * DIL + ROWS, c : c + LANES] * same
        order = channel_order(core, place_ref[1], place_ref[2])
        for c in range(0, CH, LANES):
            perm[:, c : c + LANES] = jnp.where(
                order == iota((CH, LANES), 1) + c, 1.0, 0.0
            ).astype(BF)
        own_row = own_ref[...].astype(F32)
        row_b = jnp.broadcast_to(own_row, (TOKENS, TOKENS))
        col_b = jnp.transpose(row_b, (1, 0))
        src, dst = iota((TOKENS, TOKENS), 0), iota((TOKENS, TOKENS), 1)
        earlier = jnp.where((row_b == col_b) & (src < dst), 1.0, 0.0)
        slot_row = (own_row * CAP + jnp.sum(earlier, axis=0, keepdims=True)).astype(I32)
        pick_t[...] = jnp.where(iota((SLOTS, TOKENS), 0) == slot_row, 1.0, 0.0).astype(BF)
        two = 2 * iota((TOKENS, ROWS), 0)
        pos = iota((TOKENS, ROWS), 1)
        pair[...] = jnp.where((pos == two) | (pos == two + 1), 0.5, 0.0).astype(BF)
        both_ref[:, CH:] = lax.dot_general(
            pair[...], pick_t[...], (((0,), (1,)), ((), ())), preferred_element_type=F32
        ).astype(BF)

    preact = dot(taps[0], w_ref[0]) + dot(taps[1], w_ref[1]) + dot(taps[2], w_ref[2])
    cdf = 0.5 * (1.0 + lax.erf(preact * 0.7071067811865476))
    bell = jnp.exp(-0.5 * preact * preact) * 0.3989422804014327
    own_cols = pl.ds(pl.multiple_of(j * CHUNK, CHUNK), CHUNK)
    both_ref[:, own_cols] = (cdf + preact * bell).astype(BF)
    x_own = x_ref[:, own_cols].astype(F32)
    hidden = (x_own + preact * cdf).astype(BF)
    pooled = dot(pair[...], hidden).astype(BF)
    placed_ref[...] = dot(pick_t[...], pooled).astype(BF)
    turned = nt_dot(perm[...], taps[j]).astype(BF)
    xt_mine_ref[0] = turned[:HALF]
    xt_peer_ref[0] = turned[HALF:]


def forward(place, x, peer, out, ids, own, w3):
    col = lambda j: (0, j)
    tap = lambda j: (j, 0, 0)
    halo = (DIL, CH + LANES)
    return pl.pallas_call(
        forward_kernel,
        grid=(3,),
        in_specs=[
            SMEM_SPEC, whole((ROWS, CH)), whole(halo), whole(halo), whole((1, ROWS)),
            whole((1, TOKENS)), pl.BlockSpec((3, CH, CHUNK), lambda j: (0, 0, j)),
        ],
        out_specs=[
            whole((ROWS, CH + SLOTS)), pl.BlockSpec((SLOTS, CHUNK), col),
            pl.BlockSpec((1, HALF, ROWS), tap), pl.BlockSpec((1, HALF, ROWS), tap),
            whole((2, ROWS, LANES)),
        ],
        out_shape=[
            jax.ShapeDtypeStruct((ROWS, CH + SLOTS), BF), jax.ShapeDtypeStruct((SLOTS, CH), BF),
            jax.ShapeDtypeStruct((3, HALF, ROWS), BF), jax.ShapeDtypeStruct((3, HALF, ROWS), BF),
            jax.ShapeDtypeStruct((2, ROWS, LANES), BF),
        ],
        scratch_shapes=[
            pltpu.VMEM((3, ROWS, CH), BF), pltpu.VMEM((CH, CH), BF), pltpu.VMEM((SLOTS, TOKENS), BF),
            pltpu.VMEM((TOKENS, ROWS), BF),
        ],
        compiler_params=pltpu.CompilerParams(vmem_limit_bytes=VMEM),
        name="forward",
    )(place, x, peer, out, ids, own, w3)


def grad_kernel(place_ref, ret_ref, both_ref, g_ref, edge_ref):
    g = dot(both_ref[:, CH:], ret_ref[...]) * both_ref[:, :CH].astype(F32)
    g = g.astype(BF)
    g_ref[...] = g
    edge_ref[...] = jnp.where(place_ref[0] == 0, g[:DIL], g[ROWS - DIL :])


def gradient(place, returned, both):
    return pl.pallas_call(
        grad_kernel,
        in_specs=[SMEM_SPEC] + [pl.BlockSpec(memory_space=pltpu.VMEM)] * 2,
        out_shape=[jax.ShapeDtypeStruct((ROWS, CH), BF), jax.ShapeDtypeStruct((DIL, CH), BF)],
        compiler_params=pltpu.CompilerParams(vmem_limit_bytes=VMEM),
        name="gradient",
    )(place, returned, both)


def wgrad_kernel(xt_ref, xtp_ref, g_ref, gp_ref, *outs):
    for k in range(3):
        total = dot(xt_ref[k], g_ref[...]) + dot(xtp_ref[k], gp_ref[...])
        for d in range(NX):
            outs[d][k] = total[d * PART : (d + 1) * PART].astype(BF)


def wgrad(xt, xt_peer, g, gp):
    cols = pl.BlockSpec((ROWS, CHUNK), lambda j: (0, j))
    xts = whole((3, HALF, ROWS))
    return pl.pallas_call(
        wgrad_kernel,
        grid=(CH // CHUNK,),
        in_specs=[xts, xts, cols, cols],
        out_specs=[pl.BlockSpec((3, PART, CHUNK), lambda j: (0, 0, j))] * NX,
        out_shape=[jax.ShapeDtypeStruct((3, PART, CH), BF)] * NX,
        compiler_params=pltpu.CompilerParams(vmem_limit_bytes=VMEM),
        name="wgrad",
    )(xt, xt_peer, g, gp)


def sum_kernel(*refs):
    ins, outs = refs[:NX], refs[NX:]
    total = ins[0][...].astype(F32)
    for ref in ins[1:]:
        total += ref[...].astype(F32)
    for d in range(NY):
        outs[d][...] = total[:, d * PIECE : (d + 1) * PIECE].astype(BF)


def sum_parts(parts):
    return pl.pallas_call(
        sum_kernel,
        out_shape=[jax.ShapeDtypeStruct((3, PIECE, CH), BF)] * NY,
        compiler_params=pltpu.CompilerParams(vmem_limit_bytes=VMEM),
        name="sum_parts",
    )(*parts)


def dgrad_kernel(place_ref, g_ref, gp_ref, out_ref, mask_ref, both_ref, ret_ref, w_ref, o_ref, taps):
    @pl.when(pl.program_id(0) == 0)
    def _():
        first = place_ref[0] == 0
        before = jnp.where(first, out_ref[...], gp_ref[ROWS - DIL :])
        after = jnp.where(first, gp_ref[:DIL], out_ref[...])
        g_ext = jnp.concatenate([before, g_ref[...], after], axis=0)
        for i, k in ((0, 2), (1, 0)):
            low = (2 - k) * DIL
            for c in range(0, CH, LANES):
                taps[i, :, c : c + LANES] = g_ext[low : low + ROWS, c : c + LANES] * mask_ref[i]

    total = dot(both_ref[:, CH:], ret_ref[...])
    total += nt_dot(taps[1], w_ref[0])
    total += nt_dot(g_ref[...], w_ref[1])
    total += nt_dot(taps[0], w_ref[2])
    o_ref[...] = total.astype(BF)


def dgrad(place, g, gp, out, masks, both, returned, w3):
    col = lambda j: (0, j)
    return pl.pallas_call(
        dgrad_kernel,
        grid=(CH // CHUNK,),
        in_specs=[
            SMEM_SPEC, whole((ROWS, CH)), whole((ROWS, CH)), whole((DIL, CH)),
            whole((2, ROWS, LANES)), whole((ROWS, CH + SLOTS)), pl.BlockSpec((SLOTS, CHUNK), col),
            pl.BlockSpec((3, CHUNK, CH), lambda j: (0, j, 0)),
        ],
        out_specs=pl.BlockSpec((ROWS, CHUNK), col),
        out_shape=jax.ShapeDtypeStruct((ROWS, CH), BF),
        scratch_shapes=[pltpu.VMEM((2, ROWS, CH), BF)],
        compiler_params=pltpu.CompilerParams(vmem_limit_bytes=VMEM),
        name="dgrad",
    )(place, g, gp, out, masks, both, returned, w3)


def to_peer(array):
    return lax.ppermute(array, "core", [(0, 1), (1, 0)])


def to_next_chip(array):
    last = NZ * NY * NC
    pairs = [(i, i - 1) for i in range(2, last, 2)] + [(i, i + 1) for i in range(1, last - 1, 2)]
    return lax.ppermute(array, SEQ, pairs)


def spread(pieces, axis):
    count = len(pieces)
    got = [pieces[0]]
    for d in range(1, count):
        pairs = [(i, (i + d) % count) for i in range(count)]
        got.append(lax.ppermute(pieces[d], axis, pairs))
    return got


def gather_x(array):
    me = lax.axis_index("batch")
    stacked = jnp.stack(spread([array] * NX, "batch"), axis=0)
    return [
        lax.dynamic_index_in_dim(stacked, (me - i + NX) % NX, 0, False) for i in range(NX)
    ]


def body(x, ids, owners, weight, proj, grads):
    x, ids, owners, grads = x[0], ids[0], owners[0, :, 0], grads[0, 0]
    core = lax.axis_index("core")
    first = core == 0
    place = jnp.stack([core, lax.axis_index("batch"), lax.axis_index("y")]).astype(I32)
    ids_b = ids.astype(BF)
    head = jnp.concatenate([x[:DIL], jnp.broadcast_to(ids_b[:DIL, None], (DIL, LANES))], axis=1)
    tail = jnp.concatenate([x[-DIL:], jnp.broadcast_to(ids_b[-DIL:, None], (DIL, LANES))], axis=1)
    peer_halo = to_peer(jnp.where(first, tail, head))
    out_halo = to_next_chip(jnp.where(first, head, tail))
    back = jnp.dot(grads.reshape(SLOTS, WIDE), proj.T, preferred_element_type=F32).astype(BF)
    back, peer_halo, out_halo = lax.optimization_barrier((back, peer_halo, out_halo))
    returned = lax.all_to_all(back, SEQ, 0, 0, tiled=True)
    w3 = weight.transpose(1, 0, 2)
    both, placed, xt_mine, xt_peer, masks = forward(
        place, x, peer_halo, out_halo, ids[None], owners[None], w3
    )
    xt_from = to_peer(xt_peer)
    g, edge = gradient(place, returned, both)
    g_peer = to_peer(g)
    g_out = to_next_chip(edge)
    placed, g = lax.optimization_barrier((placed, g))
    received = lax.all_to_all(placed, SEQ, 0, 0, tiled=True)
    parts = spread(wgrad(xt_mine, xt_from, g, g_peer), "batch")
    input_grad = dgrad(place, g, g_peer, g_out, masks, both, returned, w3)
    pieces = sum_parts(parts)
    pieces, input_grad = lax.optimization_barrier((pieces, input_grad))
    pieces = spread(pieces, "y")
    by_xy = sum(part.astype(F32) for part in pieces).astype(BF)
    by_xy = by_xy.reshape(3, NZ, REST, CH).transpose(1, 0, 2, 3)
    by_xy, received = lax.optimization_barrier((by_xy, received))
    owner_rows = jnp.dot(received, proj, preferred_element_type=F32).astype(BF)
    by_z = lax.all_to_all(by_xy, "z", 0, 0, tiled=True)
    by_z, owner_rows = lax.optimization_barrier((by_z, owner_rows))
    by_z = jnp.sum(by_z.astype(F32), axis=0).astype(BF)
    every = jnp.concatenate(gather_x(by_z), axis=1)
    conv_grad = every.transpose(1, 0, 2).astype(F32)
    return (
        owner_rows.reshape(1, 1, NZ * NY * NC, CAP, WIDE),
        input_grad[None],
        conv_grad,
    )


def solution(mesh):
    fine = Mesh(mesh.devices.reshape(NZ, NY, NC, NX), ("z", "y", "core", "batch"))
    return jax.shard_map(
        body,
        mesh=fine,
        in_specs=(
            P("batch", SEQ, None),
            P("batch", SEQ),
            P("batch", SEQ, None),
            P(),
            P(),
            P("batch", SEQ, None, None, None),
        ),
        out_specs=(
            P("batch", SEQ, None, None, None),
            P("batch", SEQ, None),
            P(SEQ, None, None),
        ),
        check_vma=False,
    )
```

```python
import functools

import jax
import jax.numpy as jnp
import numpy as np
from jax import lax
from jax.experimental import pallas as pl
from jax.experimental.pallas import tpu as pltpu
from jax.sharding import Mesh, PartitionSpec as P

DIL = 32
SEQ = ("z", "y", "core")
BF = jnp.bfloat16
F32 = jnp.float32
I32 = jnp.int32
LANES = 128
CHUNK = 256
NZ, NY, NC, NX = 8, 4, 2, 4
ROWS, TOKENS, SLOTS, CH, WIDE, CAP = 512, 256, 512, 768, 1536, 8
HALF = CH // 2
OWN = CH // (NZ * NY * NC)
REST = OWN // NX
PIECE = NZ * REST
PART = NY * PIECE
VMEM = 20 * 1024 * 1024
SMEM_SPEC = pl.BlockSpec(memory_space=pltpu.SMEM)


def nt_dot(a, b):
    return lax.dot_general(a, b, (((1,), (1,)), ((), ())), preferred_element_type=F32)


def tn_dot(a, b):
    return lax.dot_general(a, b, (((0,), (0,)), ((), ())), preferred_element_type=F32)


def dot(a, b):
    return jnp.dot(a, b, preferred_element_type=F32)


def whole(shape):
    return pl.BlockSpec(shape, lambda j: (0,) * len(shape))


def iota(shape, dim):
    return lax.broadcasted_iota(I32, shape, dim)


def channel_order(core, x_me, y_me):
    q = iota((CH, LANES), 0)
    other = (q >= HALF).astype(I32)
    left = q - HALF * other
    parts = []
    size = HALF
    for count in (NX, NY, NZ):
        size //= count
        digit = jnp.zeros_like(q)
        for i in range(1, count):
            digit += (left >= size * i).astype(I32)
        left = left - size * digit
        parts.append(digit)
    x, y, z = parts
    half = core + other - 2 * core * other
    y, x = y + y_me, x + x_me
    y = jnp.where(y >= NY, y - NY, y)
    x = jnp.where(x >= NX, x - NX, x)
    return z * (NY * NC * OWN) + y * (NC * OWN) + half * OWN + x * REST + left


def forward_kernel(
    place_ref, x_ref, peer_ref, out_ref, ids_ref, own_ref, w_ref,
    both_ref, placed_ref, xt_mine_ref, xt_peer_ref, mask_ref,
    taps, perm, pick_t, pair,
):
    j = pl.program_id(0)
    core = place_ref[0]

    @pl.when(j == 0)
    def _():
        first = core == 0
        before = jnp.where(first, out_ref[...], peer_ref[...])
        after = jnp.where(first, peer_ref[...], out_ref[...])
        ids_col = jnp.transpose(
            jnp.broadcast_to(ids_ref[...].astype(F32), (LANES, ROWS)), (1, 0)
        )
        ids_ext = jnp.concatenate(
            [before[:, CH:].astype(F32), ids_col, after[:, CH:].astype(F32)], axis=0
        )
        x_ext = jnp.concatenate([before[:, :CH], x_ref[...], after[:, :CH]], axis=0)
        taps[1] = x_ref[...]
        for i, k in ((0, 0), (1, 2)):
            same = jnp.where(ids_ext[k * DIL : k * DIL + ROWS] == ids_col, 1.0, 0.0).astype(BF)
            mask_ref[i] = same
            for c in range(0, CH, LANES):
                taps[k, :, c : c + LANES] = x_ext[k * DIL : k * DIL + ROWS, c : c + LANES] * same
        order = channel_order(core, place_ref[1], place_ref[2])
        for c in range(0, CH, LANES):
            perm[:, c : c + LANES] = jnp.where(
                order == iota((CH, LANES), 1) + c, 1.0, 0.0
            ).astype(BF)
        own_row = own_ref[...].astype(F32)
        row_b = jnp.broadcast_to(own_row, (TOKENS, TOKENS))
        col_b = jnp.transpose(row_b, (1, 0))
        src, dst = iota((TOKENS, TOKENS), 0), iota((TOKENS, TOKENS), 1)
        earlier = jnp.where((row_b == col_b) & (src < dst), 1.0, 0.0)
        slot_row = (own_row * CAP + jnp.sum(earlier, axis=0, keepdims=True)).astype(I32)
        pick_t[...] = jnp.where(iota((SLOTS, TOKENS), 0) == slot_row, 1.0, 0.0).astype(BF)
        two = 2 * iota((TOKENS, ROWS), 0)
        pos = iota((TOKENS, ROWS), 1)
        pair[...] = jnp.where((pos == two) | (pos == two + 1), 0.5, 0.0).astype(BF)
        both_ref[:, CH:] = lax.dot_general(
            pair[...], pick_t[...], (((0,), (1,)), ((), ())), preferred_element_type=F32
        ).astype(BF)

    preact = dot(taps[0], w_ref[0]) + dot(taps[1], w_ref[1]) + dot(taps[2], w_ref[2])
    cdf = 0.5 * (1.0 + lax.erf(preact * 0.7071067811865476))
    bell = jnp.exp(-0.5 * preact * preact) * 0.3989422804014327
    own_cols = pl.ds(pl.multiple_of(j * CHUNK, CHUNK), CHUNK)
    both_ref[:, own_cols] = (cdf + preact * bell).astype(BF)
    x_own = x_ref[:, own_cols].astype(F32)
    hidden = (x_own + preact * cdf).astype(BF)
    pooled = dot(pair[...], hidden).astype(BF)
    placed_ref[...] = dot(pick_t[...], pooled).astype(BF)
    turned = nt_dot(perm[...], taps[j]).astype(BF)
    xt_mine_ref[0] = turned[:HALF]
    xt_peer_ref[0] = turned[HALF:]


def forward(place, x, peer, out, ids, own, w3):
    col = lambda j: (0, j)
    tap = lambda j: (j, 0, 0)
    halo = (DIL, CH + LANES)
    return pl.pallas_call(
        forward_kernel,
        grid=(3,),
        in_specs=[
            SMEM_SPEC, whole((ROWS, CH)), whole(halo), whole(halo), whole((1, ROWS)),
            whole((1, TOKENS)), pl.BlockSpec((3, CH, CHUNK), lambda j: (0, 0, j)),
        ],
        out_specs=[
            whole((ROWS, CH + SLOTS)), pl.BlockSpec((SLOTS, CHUNK), col),
            pl.BlockSpec((1, HALF, ROWS), tap), pl.BlockSpec((1, HALF, ROWS), tap),
            whole((2, ROWS, LANES)),
        ],
        out_shape=[
            jax.ShapeDtypeStruct((ROWS, CH + SLOTS), BF), jax.ShapeDtypeStruct((SLOTS, CH), BF),
            jax.ShapeDtypeStruct((3, HALF, ROWS), BF), jax.ShapeDtypeStruct((3, HALF, ROWS), BF),
            jax.ShapeDtypeStruct((2, ROWS, LANES), BF),
        ],
        scratch_shapes=[
            pltpu.VMEM((3, ROWS, CH), BF), pltpu.VMEM((CH, CH), BF), pltpu.VMEM((SLOTS, TOKENS), BF),
            pltpu.VMEM((TOKENS, ROWS), BF),
        ],
        compiler_params=pltpu.CompilerParams(vmem_limit_bytes=VMEM),
        name="forward",
    )(place, x, peer, out, ids, own, w3)


def grad_kernel(place_ref, ret_ref, both_ref, g_ref, edge_ref):
    g = dot(both_ref[:, CH:], ret_ref[...]) * both_ref[:, :CH].astype(F32)
    g = g.astype(BF)
    g_ref[...] = g
    edge_ref[...] = jnp.where(place_ref[0] == 0, g[:DIL], g[ROWS - DIL :])


def gradient(place, returned, both):
    return pl.pallas_call(
        grad_kernel,
        in_specs=[SMEM_SPEC] + [pl.BlockSpec(memory_space=pltpu.VMEM)] * 2,
        out_shape=[jax.ShapeDtypeStruct((ROWS, CH), BF), jax.ShapeDtypeStruct((DIL, CH), BF)],
        compiler_params=pltpu.CompilerParams(vmem_limit_bytes=VMEM),
        name="gradient",
    )(place, returned, both)


def wgrad_kernel(xt_ref, xtp_ref, g_ref, gp_ref, *outs):
    for k in range(3):
        total = dot(xt_ref[k], g_ref[...]) + dot(xtp_ref[k], gp_ref[...])
        for d in range(NX):
            outs[d][k] = total[d * PART : (d + 1) * PART].astype(BF)


def wgrad(xt, xt_peer, g, gp, side):
    cols = pl.BlockSpec((ROWS, HALF), lambda j: (0, side))
    xts = whole((3, HALF, ROWS))
    return pl.pallas_call(
        wgrad_kernel,
        grid=(1,),
        in_specs=[xts, xts, cols, cols],
        out_specs=[whole((3, PART, HALF))] * NX,
        out_shape=[jax.ShapeDtypeStruct((3, PART, HALF), BF)] * NX,
        compiler_params=pltpu.CompilerParams(vmem_limit_bytes=VMEM),
        name="wgrad%d" % side,
    )(xt, xt_peer, g, gp)


def sum_kernel(*refs):
    outs = refs[2 * NX :]
    for side in (0, 1):
        ins = refs[side * NX : side * NX + NX]
        total = ins[0][...].astype(F32)
        for ref in ins[1:]:
            total += ref[...].astype(F32)
        for d in range(NY):
            piece = total[:, d * PIECE : (d + 1) * PIECE].astype(BF)
            outs[d][:, :, side * HALF : (side + 1) * HALF] = piece


def sum_parts(parts):
    return pl.pallas_call(
        sum_kernel,
        out_shape=[jax.ShapeDtypeStruct((3, PIECE, CH), BF)] * NY,
        compiler_params=pltpu.CompilerParams(vmem_limit_bytes=VMEM),
        name="sum_parts",
    )(*parts)


def dgrad_kernel(place_ref, g_ref, gp_ref, out_ref, mask_ref, both_ref, ret_ref, w_ref, o_ref, taps):
    @pl.when(pl.program_id(0) == 0)
    def _():
        first = place_ref[0] == 0
        before = jnp.where(first, out_ref[...], gp_ref[ROWS - DIL :])
        after = jnp.where(first, gp_ref[:DIL], out_ref[...])
        g_ext = jnp.concatenate([before, g_ref[...], after], axis=0)
        for i, k in ((0, 2), (1, 0)):
            low = (2 - k) * DIL
            for c in range(0, CH, LANES):
                taps[i, :, c : c + LANES] = g_ext[low : low + ROWS, c : c + LANES] * mask_ref[i]

    total = dot(both_ref[:, CH:], ret_ref[...])
    total += nt_dot(taps[1], w_ref[0])
    total += nt_dot(g_ref[...], w_ref[1])
    total += nt_dot(taps[0], w_ref[2])
    o_ref[...] = total.astype(BF)


def dgrad(place, g, gp, out, masks, both, returned, w3):
    col = lambda j: (0, j)
    return pl.pallas_call(
        dgrad_kernel,
        grid=(CH // CHUNK,),
        in_specs=[
            SMEM_SPEC, whole((ROWS, CH)), whole((ROWS, CH)), whole((DIL, CH)),
            whole((2, ROWS, LANES)), whole((ROWS, CH + SLOTS)), pl.BlockSpec((SLOTS, CHUNK), col),
            pl.BlockSpec((3, CHUNK, CH), lambda j: (0, j, 0)),
        ],
        out_specs=pl.BlockSpec((ROWS, CHUNK), col),
        out_shape=jax.ShapeDtypeStruct((ROWS, CH), BF),
        scratch_shapes=[pltpu.VMEM((2, ROWS, CH), BF)],
        compiler_params=pltpu.CompilerParams(vmem_limit_bytes=VMEM),
        name="dgrad",
    )(place, g, gp, out, masks, both, returned, w3)


def to_peer(array):
    return lax.ppermute(array, "core", [(0, 1), (1, 0)])


def to_next_chip(array):
    last = NZ * NY * NC
    pairs = [(i, i - 1) for i in range(2, last, 2)] + [(i, i + 1) for i in range(1, last - 1, 2)]
    return lax.ppermute(array, SEQ, pairs)


def spread(pieces, axis):
    count = len(pieces)
    got = [pieces[0]]
    for d in range(1, count):
        pairs = [(i, (i + d) % count) for i in range(count)]
        got.append(lax.ppermute(pieces[d], axis, pairs))
    return got


def gather_x(array):
    me = lax.axis_index("batch")
    stacked = jnp.stack(spread([array] * NX, "batch"), axis=0)
    return [
        lax.dynamic_index_in_dim(stacked, (me - i + NX) % NX, 0, False) for i in range(NX)
    ]


def body(x, ids, owners, weight, proj, grads):
    x, ids, owners, grads = x[0], ids[0], owners[0, :, 0], grads[0, 0]
    core = lax.axis_index("core")
    first = core == 0
    place = jnp.stack([core, lax.axis_index("batch"), lax.axis_index("y")]).astype(I32)
    ids_b = ids.astype(BF)
    head = jnp.concatenate([x[:DIL], jnp.broadcast_to(ids_b[:DIL, None], (DIL, LANES))], axis=1)
    tail = jnp.concatenate([x[-DIL:], jnp.broadcast_to(ids_b[-DIL:, None], (DIL, LANES))], axis=1)
    peer_halo = to_peer(jnp.where(first, tail, head))
    out_halo = to_next_chip(jnp.where(first, head, tail))
    back = jnp.dot(grads.reshape(SLOTS, WIDE), proj.T, preferred_element_type=F32).astype(BF)
    back, peer_halo, out_halo = lax.optimization_barrier((back, peer_halo, out_halo))
    returned = lax.all_to_all(back, SEQ, 0, 0, tiled=True)
    w3 = weight.transpose(1, 0, 2)
    both, placed, xt_mine, xt_peer, masks = forward(
        place, x, peer_halo, out_halo, ids[None], owners[None], w3
    )
    xt_from = to_peer(xt_peer)
    g, edge = gradient(place, returned, both)
    g_peer = to_peer(g)
    g_out = to_next_chip(edge)
    placed, g = lax.optimization_barrier((placed, g))
    received = lax.all_to_all(placed, SEQ, 0, 0, tiled=True)
    parts = []
    for side in (0, 1):
        parts += spread(wgrad(xt_mine, xt_from, g, g_peer, side), "batch")
    input_grad = dgrad(place, g, g_peer, g_out, masks, both, returned, w3)
    pieces = sum_parts(parts)
    pieces, input_grad = lax.optimization_barrier((pieces, input_grad))
    pieces = spread(pieces, "y")
    by_xy = sum(part.astype(F32) for part in pieces).astype(BF)
    by_xy = by_xy.reshape(3, NZ, REST, CH).transpose(1, 0, 2, 3)
    by_xy, received = lax.optimization_barrier((by_xy, received))
    owner_rows = jnp.dot(received, proj, preferred_element_type=F32).astype(BF)
    by_z = lax.all_to_all(by_xy, "z", 0, 0, tiled=True)
    by_z, owner_rows = lax.optimization_barrier((by_z, owner_rows))
    by_z = jnp.sum(by_z.astype(F32), axis=0).astype(BF)
    every = jnp.concatenate(gather_x(by_z), axis=1)
    conv_grad = every.transpose(1, 0, 2).astype(F32)
    return (
        owner_rows.reshape(1, 1, NZ * NY * NC, CAP, WIDE),
        input_grad[None],
        conv_grad,
    )


def solution(mesh):
    fine = Mesh(mesh.devices.reshape(NZ, NY, NC, NX), ("z", "y", "core", "batch"))
    return jax.shard_map(
        body,
        mesh=fine,
        in_specs=(
            P("batch", SEQ, None),
            P("batch", SEQ),
            P("batch", SEQ, None),
            P(),
            P(),
            P("batch", SEQ, None, None, None),
        ),
        out_specs=(
            P("batch", SEQ, None, None, None),
            P("batch", SEQ, None),
            P(SEQ, None, None),
        ),
        check_vma=False,
    )
```
